32 devices in a mesh: dp: 8 (over z, y), tensor: 4 (over x, core).
Axes of the slice: x: 2, y: 2, z: 4, core: 2. Of those that a mesh axis runs over, the one named last changes fastest.
Arguments:
- gradient: bfloat16 [8, 128, 8192], P('dp', None, 'tensor'), may hold values from -600 to 600
- momentum: float32 [8, 128, 8192], P('dp', None, 'tensor'), may hold values from -8 to 8
Outputs:
- new_momentum: float32 [8, 128, 8192], P('dp', None, 'tensor')
- update: float32 [128, 8192], P(None, 'tensor')
The draws below stay inside these ranges and needn't reach their ends.
All inputs are finite; a program needn't handle non-finite values.
Results may differ from the reference program's by a relative error of at most 0.0003.
Values sent between devices are 32-bit elements; how exact they have to be, the bound alone decides.
A program may use at most 64 MiB of HBM per device.

```python
import jax
import jax.numpy as jnp
from jax import lax

COLS = 8192
ROWS = 128
BLOCK = 64
KEEP = 8
REPLICAS = 8


def draw_gradient(key, part):
    key = jax.random.fold_in(key, 11)
    key_rows, key_cols, key_base = jax.random.split(key, 3)
    row_rise = jnp.exp(jnp.arange(ROWS, dtype=jnp.float32)[:, None] / ROWS * jnp.log(3.0))
    row_scale = jnp.exp(jax.random.uniform(key_rows, (ROWS, 1), jnp.float32) * jnp.log(10.0)) * row_rise
    rise = jnp.exp(jnp.arange(COLS, dtype=jnp.float32)[None, :] / COLS * jnp.log(3.0))
    col_scale = jnp.exp(jax.random.uniform(key_cols, (1, COLS), jnp.float32) * jnp.log(10.0)) * rise
    base = jax.random.truncated_normal(key_base, -6.0, 6.0, (REPLICAS, ROWS, COLS), jnp.float32)
    return (0.2 * base * row_scale * col_scale).astype(jnp.bfloat16)


def steps_of(stream_key, dims, cuts, smallest, largest):
    def one(position, blocks):
        draws = jax.random.uniform(jax.random.fold_in(jax.random.fold_in(stream_key, 6), position), (blocks,), jnp.float32, smallest / len(cuts), largest / len(cuts))
        return jnp.repeat(jnp.exp(draws), dims[position] // blocks).reshape((-1,) + (1,) * (len(dims) - position - 1))

    level = one(*cuts[0])
    for cut in cuts[1:]:
        level = level * one(*cut)
    return level


def normal_values(key, shape, scale, reach, cuts=(), held_as=jnp.bfloat16):
    result = jax.random.normal(key, shape, jnp.float32) * scale
    if len(cuts) > 0:
        result = steps_of(key, shape, cuts, -0.22, 0.18) * result
    return jnp.clip(result, min=-reach, max=reach).astype(held_as)


def setup_inputs(seed: int = 0) -> dict:
    key_list = jax.random.split(jax.random.key(seed), 3)
    gradient = draw_gradient(jax.random.fold_in(key_list[2], 71), 0)
    momentum = normal_values(key_list[1], (REPLICAS, ROWS, COLS), 2.0, 8.0, ((0, 8), (2, 4)), jnp.float32)
    return dict(gradient=gradient, momentum=momentum)


momentum_decay = 0.999

def low_basis():
    freq = jnp.arange(KEEP, dtype=jnp.float32)[:, None]
    place = jnp.arange(BLOCK, dtype=jnp.float32)[None, :]
    table = jnp.cos(jnp.pi * (2.0 * place + 1.0) * freq / (2.0 * BLOCK))
    factor = jnp.where(freq == 0.0, jnp.sqrt(1.0 / BLOCK), jnp.sqrt(2.0 / BLOCK)).astype(jnp.float32)
    return (table * factor).astype(jnp.float32)

def encode(field, basis):
    rows, cols = field.shape
    tiles = field.reshape(rows // BLOCK, BLOCK, cols // BLOCK, BLOCK)
    return jnp.einsum('ka,racb,lb->rkcl', basis, tiles, basis, precision=lax.Precision.HIGHEST)

def decode(coeffs, basis):
    nrb, keep_a, ncb, keep_b = coeffs.shape
    tiles = jnp.einsum('ka,rkcl,lb->racb', basis, coeffs, basis, precision=lax.Precision.HIGHEST)
    return tiles.reshape(nrb * BLOCK, ncb * BLOCK)

def reference(gradient, momentum):
    basis = low_basis()

    def replica(pair):
        grad_one, mom_one = pair
        accum = momentum_decay * mom_one + grad_one.astype(jnp.float32)
        coeffs = encode(accum, basis)
        return (accum - decode(coeffs, basis), coeffs)
    new_momentum, coeffs = lax.map(replica, (gradient, momentum))
    total = lax.optimization_barrier(jnp.sum(coeffs, axis=0))
    decoded = decode(total, basis)
    scale = jnp.sqrt(jnp.mean(decoded * decoded) + 1e-06)
    return (new_momentum, decoded / scale)
```

```python
import functools

import jax
import jax.numpy as jnp
import ml_dtypes
import numpy as np
from jax import lax
from jax.experimental import pallas as pl
from jax.experimental.pallas import tpu as pltpu
from jax.sharding import PartitionSpec as P

BLOCK = 64
KEEP = 8
TILE = 256
LANES = 128
GROUP = TILE // BLOCK * KEEP

momentum_decay = 0.999

BF16 = jnp.bfloat16
F32 = jnp.float32
MESH = pl.DeviceIdType.MESH


def low_basis():
    freq = np.arange(KEEP, dtype=np.float64)[:, None]
    place = np.arange(BLOCK, dtype=np.float64)[None, :]
    table = np.cos(np.pi * (2.0 * place + 1.0) * freq / (2.0 * BLOCK))
    factor = np.where(freq == 0.0, np.sqrt(1.0 / BLOCK), np.sqrt(2.0 / BLOCK))
    return (table * factor).astype(np.float32)


def halves(table):
    high = table.astype(ml_dtypes.bfloat16)
    low = (table - high.astype(np.float32)).astype(ml_dtypes.bfloat16)
    return high, low


def tables(rows):
    basis = low_basis()
    down = np.kron(np.eye(rows // BLOCK, dtype=np.float32), basis)
    across = np.kron(np.eye(TILE // BLOCK, dtype=np.float32), basis)
    dh, dl = halves(down)
    ah, al = halves(across)
    row_enc = np.concatenate([np.concatenate([dh, dh], 1), np.concatenate([dl, dl], 1)], 0)
    col_enc = np.zeros((TILE, 2 * LANES), ml_dtypes.bfloat16)
    col_enc[:, :GROUP] = ah.T
    col_enc[:, LANES:LANES + GROUP] = al.T
    col_dec = np.concatenate([ah, ah, al, al], 0)
    row_dec = np.concatenate([dh.T, dl.T, dh.T, dl.T], 1)
    parts = (row_enc, col_enc, col_dec, row_dec)
    table = np.zeros((sum(p.shape[0] for p in parts), TILE), np.float32)
    spans, at = [], 0
    for p in parts:
        table[at:at + p.shape[0], :p.shape[1]] = p.astype(np.float32)
        spans.append((at, *p.shape))
        at += p.shape[0]
    return table, spans


def split(value):
    high = value.astype(BF16)
    return high, (value - high.astype(F32)).astype(BF16)


def dot(left, right):
    return jnp.dot(left, right, preferred_element_type=F32)


def spread(coeffs, t):
    half, j = divmod(t * GROUP, LANES)
    j //= GROUP
    part = coeffs[:, half * LANES:(half + 1) * LANES]
    group = lax.broadcasted_iota(jnp.int32, part.shape, 1) // GROUP
    part = jnp.where(group == j, part, 0.0)
    part = part + pltpu.roll(part, 2 * GROUP, 1)
    part = part + pltpu.roll(part, GROUP, 1)
    high = part.astype(BF16).astype(F32)
    return jnp.where(group % 2 == 0, high, part - high).astype(BF16)


def decode_tiles(coeffs, tiles, col_dec, row_dec, emit):
    kr = coeffs.shape[0]
    left = jnp.concatenate([spread(coeffs, t) for t in range(tiles)], 0)
    wide = dot(left, col_dec)
    for t in range(tiles):
        high, low = split(wide[t * kr:(t + 1) * kr])
        emit(t, dot(row_dec, jnp.concatenate([high, high, low, low], 0)))


def exchange_kernel(n_dp, n_tp, chunks, spans, g_hbm, m_hbm, table_hbm,
                    nm_ref, out_ref, col_dec_ref, row_dec_ref, g_buf, table_buf, mine, slots, sq_slots,
                    load_sems, table_sem, send_sems, recv_sems, sq_send, sq_recv):
    rows, cols = nm_ref.shape
    kr = rows // BLOCK * KEEP
    tiles = cols // TILE
    step = cols // chunks
    table_load = pltpu.make_async_copy(table_hbm, table_buf, table_sem)
    table_load.start()
    loads = []
    for c in range(chunks):
        at = pl.ds(c * step, step)
        loads.append((
            pltpu.make_async_copy(m_hbm.at[0, :, at], nm_ref.at[:, at], load_sems.at[0, c]),
            pltpu.make_async_copy(g_hbm.at[0, :, at], g_buf.at[:, at], load_sems.at[1, c]),
        ))
        for load in loads[-1]:
            load.start()

    me = lax.axis_index("dp")
    col = lax.axis_index("tensor")
    barrier = pltpu.get_barrier_semaphore()
    for d in range(1, n_dp):
        pl.semaphore_signal(barrier, inc=1, device_id=(lax.rem(me + d, n_dp), col),
                            device_id_type=MESH)
    for d in range(1, n_tp):
        pl.semaphore_signal(barrier, inc=1, device_id=(me, lax.rem(col + d, n_tp)),
                            device_id_type=MESH)

    table_load.wait()
    row_enc, col_enc, col_dec, row_dec = (
        table_buf[at:at + r, :].astype(BF16)[:, :c] for at, r, c in spans)
    col_dec_ref[...] = col_dec
    row_dec_ref[...] = row_dec
    rows_done = []
    for t in range(tiles):
        if t * TILE % step == 0:
            for load in loads[t * TILE // step]:
                load.wait()
        at = pl.ds(t * TILE, TILE)
        accum = momentum_decay * nm_ref[:, at] + g_buf[:, at].astype(F32)
        nm_ref[:, at] = accum
        both = dot(row_enc, jnp.concatenate(split(accum), 0))
        rows_done.extend(split(both[:kr] + both[kr:]))
    both = dot(jnp.concatenate(rows_done, 0), col_enc)
    both = both[:, :LANES] + both[:, LANES:]
    per = LANES // GROUP
    parts = []
    for h in range(tiles // per):
        acc = None
        for j in range(per):
            base = (h * per + j) * 2 * kr
            part = both[base:base + kr] + both[base + kr:base + 2 * kr]
            if j:
                part = pltpu.roll(part, GROUP * j, 1)
            acc = part if acc is None else acc + part
        parts.append(acc)
    coeffs = jnp.concatenate(parts, 1)
    mine[...] = coeffs

    pl.semaphore_wait(barrier, n_dp - 1 + n_tp - 1)
    copies = []
    for d in range(1, n_dp):
        copy = pltpu.make_async_remote_copy(
            src_ref=mine, dst_ref=slots.at[me],
            send_sem=send_sems.at[d], recv_sem=recv_sems.at[d],
            device_id=(lax.rem(me + d, n_dp), col), device_id_type=MESH)
        copy.start()
        copies.append(copy)
    slots[me] = coeffs

    def remove(t, tile):
        at = pl.ds(t * TILE, TILE)
        nm_ref[:, at] = nm_ref[:, at] - tile

    decode_tiles(coeffs, tiles, col_dec, row_dec, remove)

    for copy in copies:
        copy.wait()
    total = slots[0]
    for d in range(1, n_dp):
        total = total + slots[d]
    square = total * total
    sq = None
    for r in range(0, kr, 8):
        for c in range(0, cols // KEEP, LANES):
            part = square[r:r + 8, c:c + LANES]
            sq = part if sq is None else sq + part
    sq_slots[col] = sq
    copies = []
    for d in range(1, n_tp):
        copy = pltpu.make_async_remote_copy(
            src_ref=sq_slots.at[col], dst_ref=sq_slots.at[col],
            send_sem=sq_send.at[d], recv_sem=sq_recv.at[d],
            device_id=(me, lax.rem(col + d, n_tp)), device_id_type=MESH)
        copy.start()
        copies.append(copy)
    for copy in copies:
        copy.wait()
    squares = sq_slots[0]
    for d in range(1, n_tp):
        squares = squares + sq_slots[d]
    squares = jnp.sum(jnp.sum(squares, 0, keepdims=True), 1, keepdims=True)
    scale = jnp.sqrt(squares / float(rows * cols * n_tp) + 1e-06)
    out_ref[...] = total / scale


def write_kernel(nm_ref, total_ref, col_dec, row_dec, nm_out, up_out, buf, sems):
    rows, cols = nm_ref.shape
    tiles = cols // TILE
    first = pltpu.make_async_copy(nm_ref, nm_out.at[0], sems.at[tiles])
    first.start()
    copies = []

    def store(t, tile):
        at = pl.ds(t * TILE, TILE)
        buf[:, at] = tile
        copy = pltpu.make_async_copy(buf.at[:, at], up_out.at[:, at], sems.at[t])
        copy.start()
        copies.append(copy)

    decode_tiles(total_ref[...], tiles, col_dec[...], row_dec[...], store)
    for copy in copies:
        copy.wait()
    first.wait()


def body(n_dp, n_tp, gradient, momentum):
    _, rows, cols = momentum.shape
    kr = rows // BLOCK * KEEP
    kc = cols // KEEP
    chunks = 4
    table, spans = tables(rows)
    vmem = pl.BlockSpec(memory_space=pltpu.VMEM)
    hbm = pl.BlockSpec(memory_space=pltpu.HBM)
    nm, total, col_dec, row_dec = pl.pallas_call(
        functools.partial(exchange_kernel, n_dp, n_tp, chunks, spans),
        name="encode_exchange",
        out_shape=(jax.ShapeDtypeStruct((rows, cols), F32), jax.ShapeDtypeStruct((kr, kc), F32),
                   jax.ShapeDtypeStruct(spans[2][1:], BF16), jax.ShapeDtypeStruct(spans[3][1:], BF16)),
        in_specs=[hbm, hbm, hbm],
        out_specs=(vmem,) * 4,
        scratch_shapes=[
            pltpu.VMEM((rows, cols), BF16),
            pltpu.VMEM(table.shape, F32),
            pltpu.VMEM((kr, kc), F32),
            pltpu.VMEM((n_dp, kr, kc), F32),
            pltpu.VMEM((n_tp, 8, LANES), F32),
            pltpu.SemaphoreType.DMA((2, chunks)),
            pltpu.SemaphoreType.DMA,
            pltpu.SemaphoreType.DMA((n_dp,)),
            pltpu.SemaphoreType.DMA((n_dp,)),
            pltpu.SemaphoreType.DMA((n_tp,)),
            pltpu.SemaphoreType.DMA((n_tp,)),
        ],
        compiler_params=pltpu.CompilerParams(
            collective_id=0, has_side_effects=True, vmem_limit_bytes=16 * 2**20),
    )(gradient, momentum, jnp.asarray(table))
    return pl.pallas_call(
        write_kernel,
        name="decode_write",
        out_shape=(jax.ShapeDtypeStruct((1, rows, cols), F32), jax.ShapeDtypeStruct((rows, cols), F32)),
        in_specs=[vmem] * 4,
        out_specs=(hbm, hbm),
        scratch_shapes=[
            pltpu.VMEM((rows, cols), F32),
            pltpu.SemaphoreType.DMA((cols // TILE + 1,)),
        ],
        compiler_params=pltpu.CompilerParams(vmem_limit_bytes=16 * 2**20),
    )(nm, total, col_dec, row_dec)


def solution(mesh):
    placed = (P("dp", None, "tensor"), P("dp", None, "tensor"))
    return jax.shard_map(
        functools.partial(body, mesh.shape["dp"], mesh.shape["tensor"]),
        mesh=mesh,
        in_specs=placed,
        out_specs=(P("dp", None, "tensor"), P(None, "tensor")),
        check_vma=False,
    )
```

```python
import functools

import jax
import jax.numpy as jnp
import ml_dtypes
import numpy as np
from jax import lax
from jax.experimental import pallas as pl
from jax.experimental.pallas import tpu as pltpu
from jax.sharding import PartitionSpec as P

BLOCK = 64
KEEP = 8
TILE = 256
LANES = 128
GROUP = TILE // BLOCK * KEEP

momentum_decay = 0.999

BF16 = jnp.bfloat16
F32 = jnp.float32
MESH = pl.DeviceIdType.MESH


def low_basis():
    freq = np.arange(KEEP, dtype=np.float64)[:, None]
    place = np.arange(BLOCK, dtype=np.float64)[None, :]
    table = np.cos(np.pi * (2.0 * place + 1.0) * freq / (2.0 * BLOCK))
    factor = np.where(freq == 0.0, np.sqrt(1.0 / BLOCK), np.sqrt(2.0 / BLOCK))
    return (table * factor).astype(np.float32)


def halves(table):
    high = table.astype(ml_dtypes.bfloat16)
    low = (table - high.astype(np.float32)).astype(ml_dtypes.bfloat16)
    return high, low


def tables(rows):
    basis = low_basis()
    down = np.kron(np.eye(rows // BLOCK, dtype=np.float32), basis)
    across = np.kron(np.eye(TILE // BLOCK, dtype=np.float32), basis)
    dh, dl = halves(down)
    ah, al = halves(across)
    row_enc = np.concatenate([np.concatenate([dh, dh], 1), np.concatenate([dl, dl], 1)], 0)
    col_enc = np.zeros((TILE, 2 * LANES), ml_dtypes.bfloat16)
    col_enc[:, :GROUP] = ah.T
    col_enc[:, LANES:LANES + GROUP] = al.T
    col_dec = np.concatenate([ah, ah, al, al], 0)
    row_dec = np.concatenate([dh.T, dl.T, dh.T, dl.T], 1)
    parts = (row_enc, col_enc, col_dec, row_dec)
    table = np.zeros((sum(p.shape[0] for p in parts), TILE), np.float32)
    spans, at = [], 0
    for p in parts:
        table[at:at + p.shape[0], :p.shape[1]] = p.astype(np.float32)
        spans.append((at, *p.shape))
        at += p.shape[0]
    return table, spans


def split(value):
    high = value.astype(BF16)
    return high, (value - high.astype(F32)).astype(BF16)


def dot(left, right):
    return jnp.dot(left, right, preferred_element_type=F32)


def spread(coeffs, t):
    half, j = divmod(t * GROUP, LANES)
    j //= GROUP
    part = coeffs[:, half * LANES:(half + 1) * LANES]
    group = lax.broadcasted_iota(jnp.int32, part.shape, 1) // GROUP
    part = jnp.where(group == j, part, 0.0)
    part = part + pltpu.roll(part, 2 * GROUP, 1)
    part = part + pltpu.roll(part, GROUP, 1)
    high = part.astype(BF16).astype(F32)
    return jnp.where(group % 2 == 0, high, part - high).astype(BF16)


def decode_tiles(coeffs, tiles, col_dec, row_dec, emit):
    kr = coeffs.shape[0]
    left = jnp.concatenate([spread(coeffs, t) for t in range(tiles)], 0)
    wide = dot(left, col_dec)
    for t in range(tiles):
        high, low = split(wide[t * kr:(t + 1) * kr])
        emit(t, dot(row_dec, jnp.concatenate([high, high, low, low], 0)))


def exchange_kernel(n_dp, n_tp, chunks, spans, g_hbm, m_hbm, table_hbm,
                    nm_ref, out_ref, col_dec_ref, row_dec_ref, g_buf, table_buf, mine, slots, sq_slots,
                    load_sems, table_sem, send_sems, recv_sems, sq_send, sq_recv):
    rows, cols = nm_ref.shape
    kr = rows // BLOCK * KEEP
    tiles = cols // TILE
    step = cols // chunks
    table_load = pltpu.make_async_copy(table_hbm, table_buf, table_sem)
    table_load.start()
    loads = []
    for c in range(chunks):
        at = pl.ds(c * step, step)
        loads.append((
            pltpu.make_async_copy(m_hbm.at[0, :, at], nm_ref.at[:, at], load_sems.at[0, c]),
            pltpu.make_async_copy(g_hbm.at[0, :, at], g_buf.at[:, at], load_sems.at[1, c]),
        ))
        for load in loads[-1]:
            load.start()

    me = lax.axis_index("dp")
    col = lax.axis_index("tensor")
    barrier = pltpu.get_barrier_semaphore()
    for d in range(1, n_dp):
        pl.semaphore_signal(barrier, inc=1, device_id=(lax.rem(me + d, n_dp), col),
                            device_id_type=MESH)
    for d in range(1, n_tp):
        pl.semaphore_signal(barrier, inc=1, device_id=(me, lax.rem(col + d, n_tp)),
                            device_id_type=MESH)

    table_load.wait()
    row_enc, col_enc, col_dec, row_dec = (
        table_buf[at:at + r, :].astype(BF16)[:, :c] for at, r, c in spans)
    col_dec_ref[...] = col_dec
    row_dec_ref[...] = row_dec
    rows_done = []
    for t in range(tiles):
        if t * TILE % step == 0:
            for load in loads[t * TILE // step]:
                load.wait()
        at = pl.ds(t * TILE, TILE)
        accum = momentum_decay * nm_ref[:, at] + g_buf[:, at].astype(F32)
        nm_ref[:, at] = accum
        both = dot(row_enc, jnp.concatenate(split(accum), 0))
        rows_done.extend(split(both[:kr] + both[kr:]))
    both = dot(jnp.concatenate(rows_done, 0), col_enc)
    both = both[:, :LANES] + both[:, LANES:]
    per = LANES // GROUP
    parts = []
    for h in range(tiles // per):
        acc = None
        for j in range(per):
            base = (h * per + j) * 2 * kr
            part = both[base:base + kr] + both[base + kr:base + 2 * kr]
            if j:
                part = pltpu.roll(part, GROUP * j, 1)
            acc = part if acc is None else acc + part
        parts.append(acc)
    coeffs = jnp.concatenate(parts, 1)
    mine[...] = coeffs

    pl.semaphore_wait(barrier, n_dp - 1 + n_tp - 1)
    copies = []
    for d in range(1, n_dp):
        copy = pltpu.make_async_remote_copy(
            src_ref=mine, dst_ref=slots.at[me],
            send_sem=send_sems.at[d], recv_sem=recv_sems.at[d],
            device_id=(lax.rem(me + d, n_dp), col), device_id_type=MESH)
        copy.start()
        copies.append(copy)
    slots[me] = coeffs

    def remove(t, tile):
        at = pl.ds(t * TILE, TILE)
        nm_ref[:, at] = nm_ref[:, at] - tile

    decode_tiles(coeffs, tiles, col_dec, row_dec, remove)

    for copy in copies:
        copy.wait_recv()
    total = slots[0]
    for d in range(1, n_dp):
        total = total + slots[d]
    square = total * total
    sq = None
    for r in range(0, kr, 8):
        for c in range(0, cols // KEEP, LANES):
            part = square[r:r + 8, c:c + LANES]
            sq = part if sq is None else sq + part
    sq_slots[col] = sq
    sq_copies = []
    for d in range(1, n_tp):
        copy = pltpu.make_async_remote_copy(
            src_ref=sq_slots.at[col], dst_ref=sq_slots.at[col],
            send_sem=sq_send.at[d], recv_sem=sq_recv.at[d],
            device_id=(me, lax.rem(col + d, n_tp)), device_id_type=MESH)
        copy.start()
        sq_copies.append(copy)
    for copy in sq_copies:
        copy.wait_recv()
    squares = sq_slots[0]
    for d in range(1, n_tp):
        squares = squares + sq_slots[d]
    squares = jnp.sum(jnp.sum(squares, 0, keepdims=True), 1, keepdims=True)
    scale = jnp.sqrt(squares / float(rows * cols * n_tp) + 1e-06)
    out_ref[...] = total * (1.0 / scale)
    for copy in copies + sq_copies:
        copy.wait_send()


def write_kernel(nm_ref, total_ref, col_dec, row_dec, nm_out, up_out, buf, sems):
    rows, cols = nm_ref.shape
    tiles = cols // TILE
    first = pltpu.make_async_copy(nm_ref, nm_out.at[0], sems.at[tiles])
    first.start()
    copies = []

    def store(t, tile):
        at = pl.ds(t * TILE, TILE)
        buf[:, at] = tile
        copy = pltpu.make_async_copy(buf.at[:, at], up_out.at[:, at], sems.at[t])
        copy.start()
        copies.append(copy)

    decode_tiles(total_ref[...], tiles, col_dec[...], row_dec[...], store)
    for copy in copies:
        copy.wait()
    first.wait()


def body(n_dp, n_tp, gradient, momentum):
    _, rows, cols = momentum.shape
    kr = rows // BLOCK * KEEP
    kc = cols // KEEP
    chunks = 2
    table, spans = tables(rows)
    vmem = pl.BlockSpec(memory_space=pltpu.VMEM)
    hbm = pl.BlockSpec(memory_space=pltpu.HBM)
    nm, total, col_dec, row_dec = pl.pallas_call(
        functools.partial(exchange_kernel, n_dp, n_tp, chunks, spans),
        name="encode_exchange",
        out_shape=(jax.ShapeDtypeStruct((rows, cols), F32), jax.ShapeDtypeStruct((kr, kc), F32),
                   jax.ShapeDtypeStruct(spans[2][1:], BF16), jax.ShapeDtypeStruct(spans[3][1:], BF16)),
        in_specs=[hbm, hbm, hbm],
        out_specs=(vmem,) * 4,
        scratch_shapes=[
            pltpu.VMEM((rows, cols), BF16),
            pltpu.VMEM(table.shape, F32),
            pltpu.VMEM((kr, kc), F32),
            pltpu.VMEM((n_dp, kr, kc), F32),
            pltpu.VMEM((n_tp, 8, LANES), F32),
            pltpu.SemaphoreType.DMA((2, chunks)),
            pltpu.SemaphoreType.DMA,
            pltpu.SemaphoreType.DMA((n_dp,)),
            pltpu.SemaphoreType.DMA((n_dp,)),
            pltpu.SemaphoreType.DMA((n_tp,)),
            pltpu.SemaphoreType.DMA((n_tp,)),
        ],
        compiler_params=pltpu.CompilerParams(
            collective_id=0, has_side_effects=True, vmem_limit_bytes=16 * 2**20),
    )(*(pltpu.with_memory_space_constraint(a, pltpu.HBM)
        for a in (gradient, momentum, jnp.asarray(table))))
    return pl.pallas_call(
        write_kernel,
        name="decode_write",
        out_shape=(jax.ShapeDtypeStruct((1, rows, cols), F32), jax.ShapeDtypeStruct((rows, cols), F32)),
        in_specs=[vmem] * 4,
        out_specs=(hbm, hbm),
        scratch_shapes=[
            pltpu.VMEM((rows, cols), F32),
            pltpu.SemaphoreType.DMA((cols // TILE + 1,)),
        ],
        compiler_params=pltpu.CompilerParams(vmem_limit_bytes=16 * 2**20),
    )(nm, total, col_dec, row_dec)


def solution(mesh):
    placed = (P("dp", None, "tensor"), P("dp", None, "tensor"))
    return jax.shard_map(
        functools.partial(body, mesh.shape["dp"], mesh.shape["tensor"]),
        mesh=mesh,
        in_specs=placed,
        out_specs=(P("dp", None, "tensor"), P(None, "tensor")),
        check_vma=False,
    )
```

```python
import functools

import jax
import jax.numpy as jnp
import ml_dtypes
import numpy as np
from jax import lax
from jax.experimental import pallas as pl
from jax.experimental.pallas import tpu as pltpu
from jax.sharding import PartitionSpec as P

BLOCK = 64
KEEP = 8
TILE = 256
LANES = 128
GROUP = TILE // BLOCK * KEEP

momentum_decay = 0.999

BF16 = jnp.bfloat16
F32 = jnp.float32
MESH = pl.DeviceIdType.MESH


def low_basis():
    freq = np.arange(KEEP, dtype=np.float64)[:, None]
    place = np.arange(BLOCK, dtype=np.float64)[None, :]
    table = np.cos(np.pi * (2.0 * place + 1.0) * freq / (2.0 * BLOCK))
    factor = np.where(freq == 0.0, np.sqrt(1.0 / BLOCK), np.sqrt(2.0 / BLOCK))
    return (table * factor).astype(np.float32)


def halves(table):
    high = table.astype(ml_dtypes.bfloat16)
    low = (table - high.astype(np.float32)).astype(ml_dtypes.bfloat16)
    return high, low


def tables(rows):
    basis = low_basis()
    down = np.kron(np.eye(rows // BLOCK, dtype=np.float32), basis)
    across = np.kron(np.eye(TILE // BLOCK, dtype=np.float32), basis)
    dh, dl = halves(down)
    ah, al = halves(across)
    row_enc = np.concatenate([np.concatenate([dh, dh], 1), np.concatenate([dl, dl], 1)], 0)
    col_enc = np.zeros((TILE, 2 * LANES), ml_dtypes.bfloat16)
    col_enc[:, :GROUP] = ah.T
    col_enc[:, LANES:LANES + GROUP] = al.T
    col_dec = np.concatenate([ah, ah, al, al], 0)
    row_dec = np.concatenate([dh.T, dl.T, dh.T, dl.T], 1)
    parts = (row_enc, col_enc, col_dec, row_dec)
    table = np.zeros((sum(p.shape[0] for p in parts), TILE), np.float32)
    spans, at = [], 0
    for p in parts:
        table[at:at + p.shape[0], :p.shape[1]] = p.astype(np.float32)
        spans.append((at, *p.shape))
        at += p.shape[0]
    return table, spans


def split(value):
    high = value.astype(BF16)
    return high, (value - high.astype(F32)).astype(BF16)


def dot(left, right):
    return jnp.dot(left, right, preferred_element_type=F32)


def spread(coeffs, t):
    half, j = divmod(t * GROUP, LANES)
    j //= GROUP
    part = coeffs[:, half * LANES:(half + 1) * LANES]
    group = lax.broadcasted_iota(jnp.int32, part.shape, 1) // GROUP
    part = jnp.where(group == j, part, 0.0)
    part = part + pltpu.roll(part, 2 * GROUP, 1)
    part = part + pltpu.roll(part, GROUP, 1)
    high = part.astype(BF16).astype(F32)
    return jnp.where(group % 2 == 0, high, part - high).astype(BF16)


def decode_tiles(coeffs, tiles, col_dec, row_dec, emit):
    kr = coeffs.shape[0]
    left = jnp.concatenate([spread(coeffs, t) for t in range(tiles)], 0)
    wide = dot(left, col_dec)
    for t in range(tiles):
        high, low = split(wide[t * kr:(t + 1) * kr])
        emit(t, dot(row_dec, jnp.concatenate([high, high, low, low], 0)))


def exchange_kernel(n_dp, n_tp, chunks, spans, g_hbm, m_hbm, table_hbm,
                    nm_ref, out_ref, col_dec_ref, row_dec_ref, g_buf, table_buf, mine, slots, sq_slots,
                    load_sems, table_sem, send_sems, recv_sems, sq_send, sq_recv):
    rows, cols = nm_ref.shape
    kr = rows // BLOCK * KEEP
    tiles = cols // TILE
    step = cols // chunks
    table_load = pltpu.make_async_copy(table_hbm, table_buf, table_sem)
    table_load.start()
    loads = []
    for c in range(chunks):
        at = pl.ds(c * step, step)
        loads.append((
            pltpu.make_async_copy(m_hbm.at[0, :, at], nm_ref.at[:, at], load_sems.at[0, c]),
            pltpu.make_async_copy(g_hbm.at[0, :, at], g_buf.at[:, at], load_sems.at[1, c]),
        ))
        for load in loads[-1]:
            load.start()

    me = lax.axis_index("dp")
    col = lax.axis_index("tensor")
    barrier = pltpu.get_barrier_semaphore()
    for d in range(1, n_dp):
        pl.semaphore_signal(barrier, inc=1, device_id=(lax.rem(me + d, n_dp), col),
                            device_id_type=MESH)
    for d in range(1, n_tp):
        pl.semaphore_signal(barrier, inc=1, device_id=(me, lax.rem(col + d, n_tp)),
                            device_id_type=MESH)

    table_load.wait()
    row_enc, col_enc = (table_buf[at:at + r, :].astype(BF16)[:, :c] for at, r, c in spans[:2])
    rows_done = []
    for t in range(tiles):
        if t * TILE % step == 0:
            for load in loads[t * TILE // step]:
                load.wait()
        at = pl.ds(t * TILE, TILE)
        accum = momentum_decay * nm_ref[:, at] + g_buf[:, at].astype(F32)
        nm_ref[:, at] = accum
        both = dot(row_enc, jnp.concatenate(split(accum), 0))
        rows_done.extend(split(both[:kr] + both[kr:]))
    both = dot(jnp.concatenate(rows_done, 0), col_enc)
    both = both[:, :LANES] + both[:, LANES:]
    per = LANES // GROUP
    parts = []
    for h in range(tiles // per):
        acc = None
        for j in range(per):
            base = (h * per + j) * 2 * kr
            part = both[base:base + kr] + both[base + kr:base + 2 * kr]
            if j:
                part = pltpu.roll(part, GROUP * j, 1)
            acc = part if acc is None else acc + part
        parts.append(acc)
    coeffs = jnp.concatenate(parts, 1)
    mine[...] = coeffs

    pl.semaphore_wait(barrier, n_dp - 1 + n_tp - 1)
    copies = []
    for d in range(1, n_dp):
        copy = pltpu.make_async_remote_copy(
            src_ref=mine, dst_ref=slots.at[me],
            send_sem=send_sems.at[d], recv_sem=recv_sems.at[d],
            device_id=(lax.rem(me + d, n_dp), col), device_id_type=MESH)
        copy.start()
        copies.append(copy)
    slots[me] = coeffs
    col_dec, row_dec = (table_buf[at:at + r, :].astype(BF16)[:, :c] for at, r, c in spans[2:])
    col_dec_ref[...] = col_dec
    row_dec_ref[...] = row_dec

    def remove(t, tile):
        at = pl.ds(t * TILE, TILE)
        nm_ref[:, at] = nm_ref[:, at] - tile

    decode_tiles(coeffs, tiles, col_dec, row_dec, remove)

    for copy in copies:
        copy.wait_recv()
    total = slots[0]
    for d in range(1, n_dp):
        total = total + slots[d]
    square = total * total
    sq = None
    for r in range(0, kr, 8):
        for c in range(0, cols // KEEP, LANES):
            part = square[r:r + 8, c:c + LANES]
            sq = part if sq is None else sq + part
    sq_slots[col] = sq
    sq_copies = []
    for d in range(1, n_tp):
        copy = pltpu.make_async_remote_copy(
            src_ref=sq_slots.at[col], dst_ref=sq_slots.at[col],
            send_sem=sq_send.at[d], recv_sem=sq_recv.at[d],
            device_id=(me, lax.rem(col + d, n_tp)), device_id_type=MESH)
        copy.start()
        sq_copies.append(copy)
    for copy in sq_copies:
        copy.wait_recv()
    squares = sq_slots[0]
    for d in range(1, n_tp):
        squares = squares + sq_slots[d]
    squares = jnp.sum(jnp.sum(squares, 0, keepdims=True), 1, keepdims=True)
    scale = jnp.sqrt(squares / float(rows * cols * n_tp) + 1e-06)
    out_ref[...] = total * (1.0 / scale)
    for copy in copies + sq_copies:
        copy.wait_send()


def write_kernel(nm_ref, total_ref, col_dec, row_dec, nm_out, up_out, buf, sems):
    rows, cols = nm_ref.shape
    tiles = cols // TILE
    first = pltpu.make_async_copy(nm_ref, nm_out.at[0], sems.at[tiles])
    first.start()
    copies = []

    def store(t, tile):
        at = pl.ds(t * TILE, TILE)
        buf[:, at] = tile
        copy = pltpu.make_async_copy(buf.at[:, at], up_out.at[:, at], sems.at[t])
        copy.start()
        copies.append(copy)

    decode_tiles(total_ref[...], tiles, col_dec[...], row_dec[...], store)
    for copy in copies:
        copy.wait()
    first.wait()


def body(n_dp, n_tp, gradient, momentum):
    _, rows, cols = momentum.shape
    kr = rows // BLOCK * KEEP
    kc = cols // KEEP
    chunks = 2
    table, spans = tables(rows)
    vmem = pl.BlockSpec(memory_space=pltpu.VMEM)
    hbm = pl.BlockSpec(memory_space=pltpu.HBM)
    nm, total, col_dec, row_dec = pl.pallas_call(
        functools.partial(exchange_kernel, n_dp, n_tp, chunks, spans),
        name="encode_exchange",
        out_shape=(jax.ShapeDtypeStruct((rows, cols), F32), jax.ShapeDtypeStruct((kr, kc), F32),
                   jax.ShapeDtypeStruct(spans[2][1:], BF16), jax.ShapeDtypeStruct(spans[3][1:], BF16)),
        in_specs=[hbm, hbm, hbm],
        out_specs=(vmem,) * 4,
        scratch_shapes=[
            pltpu.VMEM((rows, cols), BF16),
            pltpu.VMEM(table.shape, F32),
            pltpu.VMEM((kr, kc), F32),
            pltpu.VMEM((n_dp, kr, kc), F32),
            pltpu.VMEM((n_tp, 8, LANES), F32),
            pltpu.SemaphoreType.DMA((2, chunks)),
            pltpu.SemaphoreType.DMA,
            pltpu.SemaphoreType.DMA((n_dp,)),
            pltpu.SemaphoreType.DMA((n_dp,)),
            pltpu.SemaphoreType.DMA((n_tp,)),
            pltpu.SemaphoreType.DMA((n_tp,)),
        ],
        compiler_params=pltpu.CompilerParams(
            collective_id=0, has_side_effects=True, vmem_limit_bytes=16 * 2**20),
    )(*(pltpu.with_memory_space_constraint(a, pltpu.HBM)
        for a in (gradient, momentum, jnp.asarray(table))))
    return pl.pallas_call(
        write_kernel,
        name="decode_write",
        out_shape=(jax.ShapeDtypeStruct((1, rows, cols), F32), jax.ShapeDtypeStruct((rows, cols), F32)),
        in_specs=[vmem] * 4,
        out_specs=(hbm, hbm),
        scratch_shapes=[
            pltpu.VMEM((rows, cols), F32),
            pltpu.SemaphoreType.DMA((cols // TILE + 1,)),
        ],
        compiler_params=pltpu.CompilerParams(vmem_limit_bytes=16 * 2**20),
    )(nm, total, col_dec, row_dec)


def solution(mesh):
    placed = (P("dp", None, "tensor"), P("dp", None, "tensor"))
    return jax.shard_map(
        functools.partial(body, mesh.shape["dp"], mesh.shape["tensor"]),
        mesh=mesh,
        in_specs=placed,
        out_specs=(P("dp", None, "tensor"), P(None, "tensor")),
        check_vma=False,
    )
```

```python
import functools

import jax
import jax.numpy as jnp
import ml_dtypes
import numpy as np
from jax import lax
from jax.experimental import pallas as pl
from jax.experimental.pallas import tpu as pltpu
from jax.sharding import PartitionSpec as P

BLOCK = 64
KEEP = 8
TILE = 256
LANES = 128
GROUP = TILE // BLOCK * KEEP

momentum_decay = 0.999

BF16 = jnp.bfloat16
F32 = jnp.float32
MESH = pl.DeviceIdType.MESH


def low_basis():
    freq = np.arange(KEEP, dtype=np.float64)[:, None]
    place = np.arange(BLOCK, dtype=np.float64)[None, :]
    table = np.cos(np.pi * (2.0 * place + 1.0) * freq / (2.0 * BLOCK))
    factor = np.where(freq == 0.0, np.sqrt(1.0 / BLOCK), np.sqrt(2.0 / BLOCK))
    return (table * factor).astype(np.float32)


def halves(table):
    high = table.astype(ml_dtypes.bfloat16)
    low = (table - high.astype(np.float32)).astype(ml_dtypes.bfloat16)
    return high, low


def tables(rows):
    basis = low_basis()
    down = np.kron(np.eye(rows // BLOCK, dtype=np.float32), basis)
    across = np.kron(np.eye(TILE // BLOCK, dtype=np.float32), basis)
    dh, dl = halves(down)
    ah, al = halves(across)
    row_enc = np.concatenate([np.concatenate([dh, dh], 1), np.concatenate([dl, dl], 1)], 0)
    col_enc = np.zeros((TILE, 2 * LANES), ml_dtypes.bfloat16)
    col_enc[:, :GROUP] = ah.T
    col_enc[:, LANES:LANES + GROUP] = al.T
    col_dec = np.concatenate([ah, ah, al, al], 0)
    row_dec = np.concatenate([dh.T, dl.T, dh.T, dl.T], 1)
    parts = (row_enc, col_enc, col_dec, row_dec)
    table = np.zeros((sum(p.shape[0] for p in parts), TILE), np.float32)
    spans, at = [], 0
    for p in parts:
        table[at:at + p.shape[0], :p.shape[1]] = p.astype(np.float32)
        spans.append((at, *p.shape))
        at += p.shape[0]
    return table, spans


def split(value):
    high = value.astype(BF16)
    return high, (value - high.astype(F32)).astype(BF16)


def dot(left, right):
    return jnp.dot(left, right, preferred_element_type=F32)


def spread(coeffs, t):
    half, j = divmod(t * GROUP, LANES)
    j //= GROUP
    part = coeffs[:, half * LANES:(half + 1) * LANES]
    group = lax.broadcasted_iota(jnp.int32, part.shape, 1) // GROUP
    part = jnp.where(group == j, part, 0.0)
    part = part + pltpu.roll(part, 2 * GROUP, 1)
    part = part + pltpu.roll(part, GROUP, 1)
    high = part.astype(BF16).astype(F32)
    return jnp.where(group % 2 == 0, high, part - high).astype(BF16)


def decode_tiles(coeffs, tiles, col_dec, row_dec, emit):
    kr = coeffs.shape[0]
    left = jnp.concatenate([spread(coeffs, t) for t in range(tiles)], 0)
    wide = dot(left, col_dec)
    for t in range(tiles):
        high, low = split(wide[t * kr:(t + 1) * kr])
        emit(t, dot(row_dec, jnp.concatenate([high, high, low, low], 0)))


def exchange_kernel(n_dp, n_tp, chunks, spans, g_hbm, m_hbm, table_hbm,
                    nm_ref, out_ref, col_dec_ref, row_dec_ref, g_buf, table_buf, mine, slots, sq_slots,
                    load_sems, table_sems, send_sems, recv_sems, sq_send, sq_recv):
    rows, cols = nm_ref.shape
    kr = rows // BLOCK * KEEP
    tiles = cols // TILE
    step = cols // chunks
    first = spans[0][1]
    table_loads = [
        pltpu.make_async_copy(table_hbm.at[at], table_buf.at[at], table_sems.at[i])
        for i, at in enumerate((pl.ds(0, first), pl.ds(first, table_buf.shape[0] - first)))]
    table_loads[0].start()
    loads = []
    for c in range(chunks):
        at = pl.ds(c * step, step)
        loads.append((
            pltpu.make_async_copy(m_hbm.at[0, :, at], nm_ref.at[:, at], load_sems.at[0, c]),
            pltpu.make_async_copy(g_hbm.at[0, :, at], g_buf.at[:, at], load_sems.at[1, c]),
        ))
        for load in loads[-1]:
            load.start()

    table_loads[1].start()

    me = lax.axis_index("dp")
    col = lax.axis_index("tensor")
    upper = (2 * me) // n_dp
    barrier = pltpu.get_barrier_semaphore()
    for d in range(1, n_dp):
        pl.semaphore_signal(barrier, inc=1, device_id=(lax.rem(me + d, n_dp), col),
                            device_id_type=MESH)
    for d in range(1, n_tp):
        pl.semaphore_signal(barrier, inc=1, device_id=(me, lax.rem(col + d, n_tp)),
                            device_id_type=MESH)

    def table(i):
        at, r, c = spans[i]
        return table_buf[at:at + r, :].astype(BF16)[:, :c]

    table_loads[0].wait()
    row_enc = table(0)
    rows_done = []
    for t in range(tiles):
        if t * TILE % step == 0:
            for load in loads[t * TILE // step]:
                load.wait()
        at = pl.ds(t * TILE, TILE)
        accum = momentum_decay * nm_ref[:, at] + g_buf[:, at].astype(F32)
        nm_ref[:, at] = accum
        both = dot(row_enc, jnp.concatenate(split(accum), 0))
        rows_done.extend(split(both[:kr] + both[kr:]))
    table_loads[1].wait()
    both = dot(jnp.concatenate(rows_done, 0), table(1))
    both = both[:, :LANES] + both[:, LANES:]
    per = LANES // GROUP
    parts = []
    for h in range(tiles // per):
        acc = None
        for j in range(per):
            base = (h * per + j) * 2 * kr
            part = both[base:base + kr] + both[base + kr:base + 2 * kr]
            if j:
                part = pltpu.roll(part, GROUP * j, 1)
            acc = part if acc is None else acc + part
        parts.append(acc)
    coeffs = jnp.concatenate(parts, 1)
    mine[...] = coeffs

    pl.semaphore_wait(barrier, n_dp - 1 + n_tp - 1)
    copies = []
    for k in range(1, n_dp):
        d = upper * k + (1 - upper) * (n_dp - k)
        copy = pltpu.make_async_remote_copy(
            src_ref=mine, dst_ref=slots.at[me],
            send_sem=send_sems.at[k], recv_sem=recv_sems.at[d],
            device_id=(lax.rem(me + d, n_dp), col), device_id_type=MESH)
        copy.start()
        copies.append(copy)
    slots[me] = coeffs
    col_dec, row_dec = table(2), table(3)
    col_dec_ref[...] = col_dec
    row_dec_ref[...] = row_dec

    def remove(t, tile):
        at = pl.ds(t * TILE, TILE)
        nm_ref[:, at] = nm_ref[:, at] - tile

    decode_tiles(coeffs, tiles, col_dec, row_dec, remove)

    for d in range(1, n_dp):
        pltpu.make_async_remote_copy(
            src_ref=mine, dst_ref=slots.at[lax.rem(me + n_dp - d, n_dp)],
            send_sem=send_sems.at[d], recv_sem=recv_sems.at[d],
            device_id=(lax.rem(me + d, n_dp), col), device_id_type=MESH).wait_recv()
    total = slots[0]
    for d in range(1, n_dp):
        total = total + slots[d]
    square = total * total
    sq = None
    for r in range(0, kr, 8):
        for c in range(0, cols // KEEP, LANES):
            part = square[r:r + 8, c:c + LANES]
            sq = part if sq is None else sq + part
    sq_slots[col] = sq
    sq_copies = []
    for d in sorted(range(1, n_tp), key=lambda d: d % 2):
        copy = pltpu.make_async_remote_copy(
            src_ref=sq_slots.at[col], dst_ref=sq_slots.at[col],
            send_sem=sq_send.at[d], recv_sem=sq_recv.at[d],
            device_id=(me, lax.rem(col + d, n_tp)), device_id_type=MESH)
        copy.start()
        sq_copies.append(copy)
    for copy in sq_copies:
        copy.wait_recv()
    squares = sq_slots[0]
    for d in range(1, n_tp):
        squares = squares + sq_slots[d]
    squares = jnp.sum(jnp.sum(squares, 0, keepdims=True), 1, keepdims=True)
    scale = jnp.sqrt(squares / float(rows * cols * n_tp) + 1e-06)
    out_ref[...] = total * (1.0 / scale)
    for copy in copies + sq_copies:
        copy.wait_send()


def write_kernel(nm_ref, total_ref, col_dec, row_dec, nm_out, up_out, buf, sems):
    rows, cols = nm_ref.shape
    tiles = cols // TILE
    first = pltpu.make_async_copy(nm_ref, nm_out.at[0], sems.at[tiles])
    first.start()
    copies = []

    def store(t, tile):
        at = pl.ds(t * TILE, TILE)
        buf[:, at] = tile
        copy = pltpu.make_async_copy(buf.at[:, at], up_out.at[:, at], sems.at[t])
        copy.start()
        copies.append(copy)

    decode_tiles(total_ref[...], tiles, col_dec[...], row_dec[...], store)
    for copy in copies:
        copy.wait()
    first.wait()


def body(n_dp, n_tp, gradient, momentum):
    _, rows, cols = momentum.shape
    kr = rows // BLOCK * KEEP
    kc = cols // KEEP
    chunks = 2
    table, spans = tables(rows)
    vmem = pl.BlockSpec(memory_space=pltpu.VMEM)
    hbm = pl.BlockSpec(memory_space=pltpu.HBM)
    nm, total, col_dec, row_dec = pl.pallas_call(
        functools.partial(exchange_kernel, n_dp, n_tp, chunks, spans),
        name="encode_exchange",
        out_shape=(jax.ShapeDtypeStruct((rows, cols), F32), jax.ShapeDtypeStruct((kr, kc), F32),
                   jax.ShapeDtypeStruct(spans[2][1:], BF16), jax.ShapeDtypeStruct(spans[3][1:], BF16)),
        in_specs=[hbm, hbm, hbm],
        out_specs=(vmem,) * 4,
        scratch_shapes=[
            pltpu.VMEM((rows, cols), BF16),
            pltpu.VMEM(table.shape, F32),
            pltpu.VMEM((kr, kc), F32),
            pltpu.VMEM((n_dp, kr, kc), F32),
            pltpu.VMEM((n_tp, 8, LANES), F32),
            pltpu.SemaphoreType.DMA((2, chunks)),
            pltpu.SemaphoreType.DMA((2,)),
            pltpu.SemaphoreType.DMA((n_dp,)),
            pltpu.SemaphoreType.DMA((n_dp,)),
            pltpu.SemaphoreType.DMA((n_tp,)),
            pltpu.SemaphoreType.DMA((n_tp,)),
        ],
        compiler_params=pltpu.CompilerParams(
            collective_id=0, has_side_effects=True, vmem_limit_bytes=16 * 2**20),
    )(*(pltpu.with_memory_space_constraint(a, pltpu.HBM)
        for a in (gradient, momentum, jnp.asarray(table))))
    return pl.pallas_call(
        write_kernel,
        name="decode_write",
        out_shape=(jax.ShapeDtypeStruct((1, rows, cols), F32), jax.ShapeDtypeStruct((rows, cols), F32)),
        in_specs=[vmem] * 4,
        out_specs=(hbm, hbm),
        scratch_shapes=[
            pltpu.VMEM((rows, cols), F32),
            pltpu.SemaphoreType.DMA((cols // TILE + 1,)),
        ],
        compiler_params=pltpu.CompilerParams(vmem_limit_bytes=16 * 2**20),
    )(nm, total, col_dec, row_dec)


def solution(mesh):
    placed = (P("dp", None, "tensor"), P("dp", None, "tensor"))
    return jax.shard_map(
        functools.partial(body, mesh.shape["dp"], mesh.shape["tensor"]),
        mesh=mesh,
        in_specs=placed,
        out_specs=(P("dp", None, "tensor"), P(None, "tensor")),
        check_vma=False,
    )
```

```python
import functools

import jax
import jax.numpy as jnp
import ml_dtypes
import numpy as np
from jax import lax
from jax.experimental import pallas as pl
from jax.experimental.pallas import tpu as pltpu
from jax.sharding import PartitionSpec as P

BLOCK = 64
KEEP = 8
TILE = 256
LANES = 128
GROUP = TILE // BLOCK * KEEP

momentum_decay = 0.999

BF16 = jnp.bfloat16
F32 = jnp.float32
MESH = pl.DeviceIdType.MESH


def low_basis():
    freq = np.arange(KEEP, dtype=np.float64)[:, None]
    place = np.arange(BLOCK, dtype=np.float64)[None, :]
    table = np.cos(np.pi * (2.0 * place + 1.0) * freq / (2.0 * BLOCK))
    factor = np.where(freq == 0.0, np.sqrt(1.0 / BLOCK), np.sqrt(2.0 / BLOCK))
    return (table * factor).astype(np.float32)


def halves(table):
    high = table.astype(ml_dtypes.bfloat16)
    low = (table - high.astype(np.float32)).astype(ml_dtypes.bfloat16)
    return high, low


def tables(rows):
    basis = low_basis()
    down = np.kron(np.eye(rows // BLOCK, dtype=np.float32), basis)
    across = np.kron(np.eye(TILE // BLOCK, dtype=np.float32), basis)
    dh, dl = halves(down)
    ah, al = halves(across)
    row_enc = np.concatenate([np.concatenate([dh, dh], 1), np.concatenate([dl, dl], 1)], 0)
    col_enc = np.zeros((TILE, 2 * LANES), ml_dtypes.bfloat16)
    col_enc[:, :GROUP] = ah.T
    col_enc[:, LANES:LANES + GROUP] = al.T
    col_dec = np.concatenate([ah, ah, al, al], 0)
    row_dec = np.concatenate([dh.T, dl.T, dh.T, dl.T], 1)
    parts = (row_enc, col_enc, col_dec, row_dec)
    table = np.zeros((sum(p.shape[0] for p in parts), TILE), np.float32)
    spans, at = [], 0
    for p in parts:
        table[at:at + p.shape[0], :p.shape[1]] = p.astype(np.float32)
        spans.append((at, *p.shape))
        at += p.shape[0]
    return table, spans


def split(value):
    high = value.astype(BF16)
    return high, (value - high.astype(F32)).astype(BF16)


def dot(left, right):
    return jnp.dot(left, right, preferred_element_type=F32)


def spread(coeffs, t):
    half, j = divmod(t * GROUP, LANES)
    j //= GROUP
    part = coeffs[:, half * LANES:(half + 1) * LANES]
    group = lax.broadcasted_iota(jnp.int32, part.shape, 1) // GROUP
    part = jnp.where(group == j, part, 0.0)
    part = part + pltpu.roll(part, 2 * GROUP, 1)
    part = part + pltpu.roll(part, GROUP, 1)
    high = part.astype(BF16).astype(F32)
    return jnp.where(group % 2 == 0, high, part - high).astype(BF16)


def decode_tiles(coeffs, tiles, col_dec, row_dec, emit):
    kr = coeffs.shape[0]
    left = jnp.concatenate([spread(coeffs, t) for t in range(tiles)], 0)
    wide = dot(left, col_dec)
    for t in range(tiles):
        high, low = split(wide[t * kr:(t + 1) * kr])
        emit(t, dot(row_dec, jnp.concatenate([high, high, low, low], 0)))


def exchange_kernel(n_dp, n_tp, chunks, spans, g_hbm, m_hbm, table_hbm,
                    nm_ref, out_ref, col_dec_ref, row_dec_ref, g_buf, table_buf, mine, slots, sq_slots,
                    load_sems, table_sems, send_sems, recv_sems, sq_send, sq_recv):
    rows, cols = nm_ref.shape
    kr = rows // BLOCK * KEEP
    tiles = cols // TILE
    step = cols // chunks
    first = spans[0][1]
    table_loads = [
        pltpu.make_async_copy(table_hbm.at[at], table_buf.at[at], table_sems.at[i])
        for i, at in enumerate((pl.ds(0, first), pl.ds(first, table_buf.shape[0] - first)))]
    table_loads[0].start()
    loads = []
    for c in range(chunks):
        at = pl.ds(c * step, step)
        loads.append((
            pltpu.make_async_copy(m_hbm.at[0, :, at], nm_ref.at[:, at], load_sems.at[0, c]),
            pltpu.make_async_copy(g_hbm.at[0, :, at], g_buf.at[:, at], load_sems.at[1, c]),
        ))
        for load in loads[-1]:
            load.start()

    me = lax.axis_index("dp")
    col = lax.axis_index("tensor")
    upper = (2 * me) // n_dp
    barrier = pltpu.get_barrier_semaphore()
    for k in range(1, n_dp):
        d = upper * k + (1 - upper) * (n_dp - k)
        pl.semaphore_signal(barrier, inc=1, device_id=(lax.rem(me + d, n_dp), col),
                            device_id_type=MESH)
    for d in range(1, n_tp):
        pl.semaphore_signal(barrier, inc=1, device_id=(me, lax.rem(col + d, n_tp)),
                            device_id_type=MESH)

    table_loads[1].start()

    def table(i):
        at, r, c = spans[i]
        return table_buf[at:at + r, :].astype(BF16)[:, :c]

    table_loads[0].wait()
    row_enc = table(0)
    rows_done = []
    for t in range(tiles):
        if t * TILE % step == 0:
            for load in loads[t * TILE // step]:
                load.wait()
        at = pl.ds(t * TILE, TILE)
        accum = momentum_decay * nm_ref[:, at] + g_buf[:, at].astype(F32)
        nm_ref[:, at] = accum
        both = dot(row_enc, jnp.concatenate(split(accum), 0))
        rows_done.extend(split(both[:kr] + both[kr:]))
    table_loads[1].wait()
    both = dot(jnp.concatenate(rows_done, 0), table(1))
    both = both[:, :LANES] + both[:, LANES:]
    per = LANES // GROUP
    parts = []
    for h in range(tiles // per):
        acc = None
        for j in range(per):
            base = (h * per + j) * 2 * kr
            part = both[base:base + kr] + both[base + kr:base + 2 * kr]
            if j:
                part = pltpu.roll(part, GROUP * j, 1)
            acc = part if acc is None else acc + part
        parts.append(acc)
    coeffs = jnp.concatenate(parts, 1)
    mine[...] = coeffs

    pl.semaphore_wait(barrier, n_dp - 1 + n_tp - 1)
    copies = []
    for k in range(1, n_dp):
        d = upper * k + (1 - upper) * (n_dp - k)
        copy = pltpu.make_async_remote_copy(
            src_ref=mine, dst_ref=slots.at[me],
            send_sem=send_sems.at[k], recv_sem=recv_sems.at[d],
            device_id=(lax.rem(me + d, n_dp), col), device_id_type=MESH)
        copy.start()
        copies.append(copy)
    slots[me] = coeffs
    col_dec, row_dec = table(2), table(3)
    col_dec_ref[...] = col_dec
    row_dec_ref[...] = row_dec

    def remove(t, tile):
        at = pl.ds(t * TILE, TILE)
        nm_ref[:, at] = nm_ref[:, at] - tile

    decode_tiles(coeffs, tiles, col_dec, row_dec, remove)

    for d in range(1, n_dp):
        pltpu.make_async_remote_copy(
            src_ref=mine, dst_ref=slots.at[lax.rem(me + n_dp - d, n_dp)],
            send_sem=send_sems.at[d], recv_sem=recv_sems.at[d],
            device_id=(lax.rem(me + d, n_dp), col), device_id_type=MESH).wait_recv()
    total = slots[0]
    for d in range(1, n_dp):
        total = total + slots[d]
    square = total * total
    sq = None
    for r in range(0, kr, 8):
        for c in range(0, cols // KEEP, LANES):
            part = square[r:r + 8, c:c + LANES]
            sq = part if sq is None else sq + part
    sq_slots[col] = sq
    sq_copies = []
    for d in sorted(range(1, n_tp), key=lambda d: d % 2):
        copy = pltpu.make_async_remote_copy(
            src_ref=sq_slots.at[col], dst_ref=sq_slots.at[col],
            send_sem=sq_send.at[d], recv_sem=sq_recv.at[d],
            device_id=(me, lax.rem(col + d, n_tp)), device_id_type=MESH)
        copy.start()
        sq_copies.append(copy)
    for copy in sq_copies:
        copy.wait_recv()
    squares = sq_slots[0]
    for d in range(1, n_tp):
        squares = squares + sq_slots[d]
    squares = jnp.sum(jnp.sum(squares, 0, keepdims=True), 1, keepdims=True)
    scale = jnp.sqrt(squares / float(rows * cols * n_tp) + 1e-06)
    out_ref[...] = total * (1.0 / scale)
    for copy in copies + sq_copies:
        copy.wait_send()


def write_kernel(nm_ref, total_ref, col_dec, row_dec, nm_out, up_out, buf, sems):
    rows, cols = nm_ref.shape
    tiles = cols // TILE
    first = pltpu.make_async_copy(nm_ref, nm_out.at[0], sems.at[tiles])
    first.start()
    copies = []

    def store(t, tile):
        at = pl.ds(t * TILE, TILE)
        buf[:, at] = tile
        copy = pltpu.make_async_copy(buf.at[:, at], up_out.at[:, at], sems.at[t])
        copy.start()
        copies.append(copy)

    decode_tiles(total_ref[...], tiles, col_dec[...], row_dec[...], store)
    for copy in copies:
        copy.wait()
    first.wait()


def body(n_dp, n_tp, gradient, momentum):
    _, rows, cols = momentum.shape
    kr = rows // BLOCK * KEEP
    kc = cols // KEEP
    chunks = 2
    table, spans = tables(rows)
    vmem = pl.BlockSpec(memory_space=pltpu.VMEM)
    hbm = pl.BlockSpec(memory_space=pltpu.HBM)
    nm, total, col_dec, row_dec = pl.pallas_call(
        functools.partial(exchange_kernel, n_dp, n_tp, chunks, spans),
        name="encode_exchange",
        out_shape=(jax.ShapeDtypeStruct((rows, cols), F32), jax.ShapeDtypeStruct((kr, kc), F32),
                   jax.ShapeDtypeStruct(spans[2][1:], BF16), jax.ShapeDtypeStruct(spans[3][1:], BF16)),
        in_specs=[hbm, hbm, hbm],
        out_specs=(vmem,) * 4,
        scratch_shapes=[
            pltpu.VMEM((rows, cols), BF16),
            pltpu.VMEM(table.shape, F32),
            pltpu.VMEM((kr, kc), F32),
            pltpu.VMEM((n_dp, kr, kc), F32),
            pltpu.VMEM((n_tp, 8, LANES), F32),
            pltpu.SemaphoreType.DMA((2, chunks)),
            pltpu.SemaphoreType.DMA((2,)),
            pltpu.SemaphoreType.DMA((n_dp,)),
            pltpu.SemaphoreType.DMA((n_dp,)),
            pltpu.SemaphoreType.DMA((n_tp,)),
            pltpu.SemaphoreType.DMA((n_tp,)),
        ],
        compiler_params=pltpu.CompilerParams(
            collective_id=0, has_side_effects=True, vmem_limit_bytes=16 * 2**20),
    )(*(pltpu.with_memory_space_constraint(a, pltpu.HBM)
        for a in (gradient, momentum, jnp.asarray(table))))
    return pl.pallas_call(
        write_kernel,
        name="decode_write",
        out_shape=(jax.ShapeDtypeStruct((1, rows, cols), F32), jax.ShapeDtypeStruct((rows, cols), F32)),
        in_specs=[vmem] * 4,
        out_specs=(hbm, hbm),
        scratch_shapes=[
            pltpu.VMEM((rows, cols), F32),
            pltpu.SemaphoreType.DMA((cols // TILE + 1,)),
        ],
        compiler_params=pltpu.CompilerParams(vmem_limit_bytes=16 * 2**20),
    )(nm, total, col_dec, row_dec)


def solution(mesh):
    placed = (P("dp", None, "tensor"), P("dp", None, "tensor"))
    return jax.shard_map(
        functools.partial(body, mesh.shape["dp"], mesh.shape["tensor"]),
        mesh=mesh,
        in_specs=placed,
        out_specs=(P("dp", None, "tensor"), P(None, "tensor")),
        check_vma=False,
    )
```
